32 devices in a mesh: dp: 8 (over y, x, core), col: 4 (over z).
Axes of the slice: x: 2, y: 2, z: 4, core: 2. Of those that a mesh axis runs over, the one named last changes fastest.
Arguments:
- activ: bfloat16 [2048, 8192], P('dp'), may hold values from -6 to 6
- grad_out: bfloat16 [2048, 26624], P('dp', 'col'), may hold values from -0.125 to 0.125
- signs: int32 [32768], P('col'), may hold values from -1 to 1, as said below
- kept: int32 [512], replicated, may hold values from 0 to 32767, as said below
Outputs:
- sketch: float32 [8192, 512], P('dp', 'col')
- projection: float32 [512, 26624], P('dp', 'col')
The draws below stay inside these ranges and needn't reach their ends.
Inputs may be any that keep to these rules, and one draw needn't show every extreme that they name: `signs`: each entry is +1 or -1. `kept`: the 512 indices are distinct.
All inputs are finite; a program needn't handle non-finite values.
Results may differ from the reference program's by a relative error of at most 0.0095.
Values may be sent and summed in bfloat16 or wider, within the bound.
A program may use at most 256 MiB of HBM per device.

```python
import math
import jax
import jax.numpy as jnp
from jax import lax

FF = 26624
ROWS = 8192
COLS = 32768
KEEP = 512
TOK_DEV = 256
TOKENS = 2048
N_DP = 8
N_COL = 4


def draw_signs(key, part):
    return (2 * jax.random.randint(key, (COLS,), 0, 2) - 1).astype(jnp.int32)


def draw_kept(key, part):
    middle = jax.random.permutation(jax.random.fold_in(key, 1), COLS - 2)[:KEEP - 2] + 1
    ends = jnp.array([0, COLS - 1], jnp.int32)
    joined = jnp.concatenate([ends, middle.astype(jnp.int32)])
    return jax.random.permutation(jax.random.fold_in(key, 2), joined).astype(jnp.int32)


def block_scale(stream_key, dims, split, low, largest):
    level, own = 1.0, jax.random.fold_in(stream_key, 6)
    for axis_at, shards_of in split:
        heights = jnp.exp(jax.random.uniform(jax.random.fold_in(own, axis_at), (shards_of,), jnp.float32, low / len(split), largest / len(split)))
        level = level * jnp.repeat(heights, dims[axis_at] // shards_of).reshape([-1 if axis == axis_at else 1 for axis in range(len(dims))])
    return level


def noise(key, dims, scale, limit, shards=(), kind=jnp.bfloat16):
    values = scale * jax.random.normal(key, dims, jnp.float32)
    if shards:
        values = values * block_scale(key, dims, shards, -0.22, 0.18)
    return jnp.clip(values, -limit, limit).astype(kind)


def setup_inputs(seed: int = 0) -> dict:
    splits = jax.random.split(jax.random.key(seed), 5)
    return {
        "activ": noise(splits[0], (TOKENS, ROWS), 1.0, 6.0, ((0, 8),)),
        "grad_out": noise(splits[1], (TOKENS, FF), TOKENS ** -0.5, 0.125, ((0, 8), (1, 4))),
        "signs": draw_signs(jax.random.fold_in(splits[4], 71), 0),
        "kept": draw_kept(jax.random.fold_in(splits[4], 71), 0),
    }


def transform_block(block, signs, kept):
    rows_here = block.shape[0]
    ff_dev = FF // N_COL
    col_dev = COLS // N_COL
    padded = jnp.pad(block.reshape(rows_here, N_COL, ff_dev), ((0, 0), (0, 0), (0, col_dev - ff_dev)))
    values = padded.reshape(rows_here, COLS) * signs.astype(jnp.float32)[None, :]
    half_len = 1
    while half_len < COLS:
        shaped = values.reshape(rows_here, COLS // (2 * half_len), 2, half_len)
        left_part = shaped[:, :, 0]
        right_part = shaped[:, :, 1]
        values = jnp.stack([left_part + right_part, left_part - right_part], axis=2).reshape(rows_here, COLS)
        half_len = half_len * 2
    return jnp.take(values, kept, axis=1) * (1.0 / math.sqrt(COLS))

def reference(activ, grad_out, signs, kept):
    groups_act = activ.reshape(N_DP, TOK_DEV, ROWS)
    groups_grad = grad_out.reshape(N_DP, TOK_DEV, FF)

    def add_group(total, pair):
        act_group, grad_group = pair
        partial_grad = jnp.dot(act_group.T.astype(jnp.float32), grad_group.astype(jnp.float32), preferred_element_type=jnp.float32).astype(jnp.bfloat16)
        return (total + partial_grad.astype(jnp.float32), None)
    gradient, unused = lax.scan(add_group, jnp.zeros((ROWS, FF), jnp.float32), (groups_act, groups_grad))
    block_rows = math.gcd(ROWS, 512)
    blocks = gradient.reshape(ROWS // block_rows, block_rows, FF)
    sketch = lax.map(lambda block: transform_block(block, signs, kept), blocks).reshape(ROWS, KEEP)
    gram_matrix = jnp.dot(sketch.T, sketch, precision=lax.Precision.HIGHEST)
    shift_size = 0.05 * jnp.trace(gram_matrix) / KEEP
    shifted = gram_matrix + shift_size * jnp.eye(KEEP, dtype=jnp.float32)
    chol_factor = jnp.linalg.cholesky(shifted)
    basis_rows = jax.scipy.linalg.solve_triangular(chol_factor, sketch.T, lower=True).T
    projection = jnp.dot(basis_rows.T, gradient, precision=lax.Precision.HIGHEST)
    return (sketch, projection)
```

```python
import math

import jax
import jax.numpy as jnp
from jax import lax
from jax.experimental import pallas as pl
from jax.experimental.pallas import tpu as pltpu
from jax.sharding import PartitionSpec as P

HI = lax.Precision.HIGHEST


def dot_hi(left, right, dims):
    return lax.dot_general(left, right, (dims, ((), ())), precision=HI,
                           preferred_element_type=jnp.float32)


def factor_block(both_ref):
    size = both_ref.shape[0]
    lane = lax.broadcasted_iota(jnp.int32, (8, size), 1)
    sub = lax.broadcasted_iota(jnp.int32, (8, size), 0)

    for p in range(size // 8):
        lo = 8 * p
        rows = both_ref[lo:lo + 8, :]
        rw, rv = rows[:, :size], rows[:, size:]
        cols = [jnp.broadcast_to(rw[:, lo + a:lo + a + 1], (8, size)) for a in range(8)]
        for a in range(8):
            pivot = jnp.broadcast_to(cols[a][a:a + 1, :], (8, size))
            root = lax.rsqrt(pivot)
            mult = jnp.where(sub > a, cols[a] * (root * root), jnp.where(sub == a, 1.0 - root, 0.0))
            for b in range(a + 1, 8):
                cols[b] = cols[b] - mult * jnp.broadcast_to(cols[b][a:a + 1, :], (8, size))
            rw = rw - mult * jnp.broadcast_to(rw[a:a + 1, :], (8, size))
            rv = rv - mult * jnp.broadcast_to(rv[a:a + 1, :], (8, size))
        done = jnp.concatenate([rw, rv], axis=1)
        both_ref[lo:lo + 8, :] = done
        if lo + 8 < size:
            left = jnp.where(lane >= lo + 8, rw, 0.0)
            step = dot_hi(left, done, ((0,), (0,)))
            both_ref[lo + 8:, :] = both_ref[lo + 8:, :] - step[lo + 8:, :]


def inverse_factor_kernel(gram_ref, out_ref, work, both):
    count = gram_ref.shape[0]
    size = both.shape[0]
    blocks = count // size
    row = lax.broadcasted_iota(jnp.int32, (count, count), 0)
    col = lax.broadcasted_iota(jnp.int32, (count, count), 1)
    gram = gram_ref[...]
    trace = jnp.sum(jnp.where(row == col, gram, 0.0))
    work[...] = gram + jnp.where(row == col, 0.05 * trace / count, 0.0)
    out_ref[...] = jnp.zeros_like(out_ref)
    eye = (lax.broadcasted_iota(jnp.int32, (size, size), 0)
           == lax.broadcasted_iota(jnp.int32, (size, size), 1)).astype(jnp.float32)
    for k in range(blocks):
        lo, hi = k * size, (k + 1) * size
        both[:, :size] = work[lo:hi, lo:hi]
        both[:, size:] = eye
        factor_block(both)
        inv = both[:, size:]
        if k:
            out_ref[lo:hi, :lo] = dot_hi(inv, out_ref[lo:hi, :lo], ((1,), (0,)))
        out_ref[lo:hi, lo:hi] = inv
        if hi < count:
            panel = dot_hi(inv, work[lo:hi, hi:], ((1,), (0,)))
            work[hi:, hi:] = work[hi:, hi:] - dot_hi(panel, panel, ((0,), (0,)))
            out_ref[hi:, :hi] = out_ref[hi:, :hi] - dot_hi(panel, out_ref[lo:hi, :hi], ((0,), (0,)))


def inverse_factor(gram):
    count = gram.shape[0]
    size = 128
    return pl.pallas_call(
        inverse_factor_kernel,
        out_shape=jax.ShapeDtypeStruct((count, count), jnp.float32),
        in_specs=[pl.BlockSpec(memory_space=pltpu.VMEM)],
        out_specs=pl.BlockSpec(memory_space=pltpu.VMEM),
        scratch_shapes=[pltpu.VMEM((count, count), jnp.float32),
                        pltpu.VMEM((size, 2 * size), jnp.float32)],
        compiler_params=pltpu.CompilerParams(vmem_limit_bytes=32 * 1024 * 1024),
        cost_estimate=pl.CostEstimate(flops=10**9, bytes_accessed=2 * 10**6, transcendentals=4096),
    )(gram)


def parity_sign(common, num_bits):
    parity = jnp.zeros_like(common)
    for shift_bit in range(num_bits):
        parity = parity + jnp.bitwise_and(jnp.right_shift(common, shift_bit), 1)
    return (1 - 2 * jnp.bitwise_and(parity, 1)).astype(jnp.bfloat16)


def kept_columns(signs, kept, my_col, ff_dev, col_dev, total_cols):
    num_bits = total_cols.bit_length() - 1
    inner = math.gcd(ff_dev, 128)
    outer = ff_dev // inner
    start = my_col * col_dev + inner * lax.broadcasted_iota(jnp.int32, (outer, 1), 0)
    high = parity_sign(jnp.bitwise_and(start, kept[None, :]), num_bits)
    place = lax.broadcasted_iota(jnp.int32, (inner, 1), 0)
    low = parity_sign(jnp.bitwise_and(place, kept[None, :]), num_bits)
    own = signs[:ff_dev].astype(jnp.bfloat16).reshape(outer, inner, 1)
    return (high[:, None, :] * low[None, :, :] * own).reshape(ff_dev, kept.shape[0])


def split(values):
    top = values.astype(jnp.bfloat16)
    return top, (values - top.astype(jnp.float32)).astype(jnp.bfloat16)


def dot_f32(left, right, dims):
    return lax.dot_general(left, right, (dims, ((), ())), preferred_element_type=jnp.float32)


def per_device(activ, grad_out, signs, kept):
    col_count = lax.axis_size("col")
    my_col = lax.axis_index("col")
    ff_dev = grad_out.shape[1]
    col_dev = signs.shape[0]
    total_cols = col_dev * col_count
    highest = lax.Precision.HIGHEST
    mine = lax.all_to_all(activ, "dp", split_axis=1, concat_axis=0, tiled=True)
    columns = kept_columns(signs, kept, my_col, ff_dev, col_dev, total_cols)
    mixed = dot_f32(grad_out, columns, ((1,), (0,))) * (1.0 / math.sqrt(total_cols))
    mixed = lax.psum_scatter(mixed, "col", scatter_dimension=1, tiled=True)
    mixed = lax.all_gather(mixed, "dp", axis=0, tiled=True)
    top, rest = split(mixed)
    sketch = dot_f32(mine, top, ((0,), (0,))) + dot_f32(mine, rest, ((0,), (0,)))
    full_rows = lax.all_gather(sketch, "col", axis=1, tiled=True)
    gram_matrix = lax.psum(jnp.dot(full_rows.T, full_rows, precision=highest), "dp")
    top, rest = split(sketch)
    back = dot_f32(mine, top, ((1,), (0,))) + dot_f32(mine, rest, ((1,), (0,)))
    back = lax.psum_scatter(back, "dp", scatter_dimension=0, tiled=True)
    back = lax.all_gather(back, "col", axis=1, tiled=True)
    solved = dot_hi(inverse_factor(gram_matrix), back, ((1,), (1,)))
    top, rest = split(solved)
    part = dot_f32(top, grad_out, ((1,), (0,))) + dot_f32(rest, grad_out, ((1,), (0,)))
    projection = lax.psum_scatter(
        part.astype(jnp.bfloat16), "dp", scatter_dimension=0, tiled=True
    ).astype(jnp.float32)
    return (sketch, projection)


def solution(mesh):
    placed = (P("dp", None), P("dp", "col"), P("col"), P())
    return jax.shard_map(
        per_device,
        mesh=mesh,
        in_specs=placed,
        out_specs=(P("dp", "col"), P("dp", "col")),
        check_vma=False,
    )
```

```python
import functools
import math

import jax
import jax.numpy as jnp
from jax import lax
from jax.experimental import pallas as pl
from jax.experimental.pallas import tpu as pltpu
from jax.sharding import PartitionSpec as P

HI = lax.Precision.HIGHEST


def dot_hi(left, right, dims):
    return lax.dot_general(left, right, (dims, ((), ())), precision=HI,
                           preferred_element_type=jnp.float32)


def factor_block(both_ref):
    size = both_ref.shape[0]
    lane = lax.broadcasted_iota(jnp.int32, (8, size), 1)
    sub = lax.broadcasted_iota(jnp.int32, (8, size), 0)

    for p in range(size // 8):
        lo = 8 * p
        rows = both_ref[lo:lo + 8, :]
        rw, rv = rows[:, :size], rows[:, size:]
        cols = [jnp.broadcast_to(rw[:, lo + a:lo + a + 1], (8, size)) for a in range(8)]
        for a in range(8):
            pivot = jnp.broadcast_to(cols[a][a:a + 1, :], (8, size))
            root = lax.rsqrt(pivot)
            mult = jnp.where(sub > a, cols[a] * (root * root), jnp.where(sub == a, 1.0 - root, 0.0))
            for b in range(a + 1, 8):
                cols[b] = cols[b] - mult * jnp.broadcast_to(cols[b][a:a + 1, :], (8, size))
            rw = rw - mult * jnp.broadcast_to(rw[a:a + 1, :], (8, size))
            rv = rv - mult * jnp.broadcast_to(rv[a:a + 1, :], (8, size))
        done = jnp.concatenate([rw, rv], axis=1)
        both_ref[lo:lo + 8, :] = done
        if lo + 8 < size:
            left = jnp.where(lane >= lo + 8, rw, 0.0)
            step = dot_hi(left, done, ((0,), (0,)))
            both_ref[lo + 8:, :] = both_ref[lo + 8:, :] - step[lo + 8:, :]


def inverse_factor_kernel(gram_ref, out_ref, work, both):
    count = gram_ref.shape[0]
    size = both.shape[0]
    blocks = count // size
    row = lax.broadcasted_iota(jnp.int32, (count, count), 0)
    col = lax.broadcasted_iota(jnp.int32, (count, count), 1)
    gram = gram_ref[...]
    trace = jnp.sum(jnp.where(row == col, gram, 0.0))
    work[...] = gram + jnp.where(row == col, 0.05 * trace / count, 0.0)
    out_ref[...] = jnp.zeros_like(out_ref)
    eye = (lax.broadcasted_iota(jnp.int32, (size, size), 0)
           == lax.broadcasted_iota(jnp.int32, (size, size), 1)).astype(jnp.float32)
    for k in range(blocks):
        lo, hi = k * size, (k + 1) * size
        both[:, :size] = work[lo:hi, lo:hi]
        both[:, size:] = eye
        factor_block(both)
        inv = both[:, size:]
        if k:
            out_ref[lo:hi, :lo] = dot_hi(inv, out_ref[lo:hi, :lo], ((1,), (0,)))
        out_ref[lo:hi, lo:hi] = inv
        if hi < count:
            panel = dot_hi(inv, work[lo:hi, hi:], ((1,), (0,)))
            work[hi:, hi:] = work[hi:, hi:] - dot_hi(panel, panel, ((0,), (0,)))
            out_ref[hi:, :hi] = out_ref[hi:, :hi] - dot_hi(panel, out_ref[lo:hi, :hi], ((0,), (0,)))


def inverse_factor(gram):
    count = gram.shape[0]
    size = 128
    return pl.pallas_call(
        inverse_factor_kernel,
        out_shape=jax.ShapeDtypeStruct((count, count), jnp.float32),
        in_specs=[pl.BlockSpec(memory_space=pltpu.VMEM)],
        out_specs=pl.BlockSpec(memory_space=pltpu.VMEM),
        scratch_shapes=[pltpu.VMEM((count, count), jnp.float32),
                        pltpu.VMEM((size, 2 * size), jnp.float32)],
        compiler_params=pltpu.CompilerParams(vmem_limit_bytes=32 * 1024 * 1024),
        cost_estimate=pl.CostEstimate(flops=10**9, bytes_accessed=2 * 10**6, transcendentals=4096),
    )(gram)


MESH = pl.DeviceIdType.MESH
SPACE = 48 * 1024 * 1024


def others(axis, count, stride=1):
    me = lax.axis_index(axis)
    total = count * stride
    for offset in range(1, count):
        yield offset, lax.rem(me + offset * stride, total)


def greet(groups):
    barrier = pltpu.get_barrier_semaphore()
    waits = 0
    for axis, count, stride in groups:
        for _, target in others(axis, count, stride):
            pl.semaphore_signal(barrier, inc=1, device_id={axis: target}, device_id_type=MESH)
            waits += 1
    pl.semaphore_wait(barrier, waits)


def send(source, target_ref, send_sem, recv_sem, axis, target):
    copy = pltpu.make_async_remote_copy(
        src_ref=source, dst_ref=target_ref, send_sem=send_sem, recv_sem=recv_sem,
        device_id={axis: target}, device_id_type=MESH)
    copy.start()
    return copy


def wait_all(copies):
    for copy in copies:
        copy.wait()


def total_of(ref, count):
    total = ref[0].astype(jnp.float32)
    for index in range(1, count):
        total = total + ref[index].astype(jnp.float32)
    return total


def first_kernel(n_dp, n_col, act_ref, part_ref, mine_ref, all_ref, landed, own, sa, ra, sc, rc, sd, rd, local_sem):
    my_dp, my_col = lax.axis_index("dp"), lax.axis_index("col")
    wide = mine_ref.shape[2]
    greet([("dp", n_dp, 1), ("col", n_col, 1)])

    def rows_of(device):
        return act_ref.at[:, pl.ds(pl.multiple_of(device * wide, wide), wide)]

    partial = [send(part_ref.at[target], landed.at[my_col], sc.at[k], rc.at[k], "col", target)
               for k, target in others("col", n_col)]
    rows = [send(rows_of(target), mine_ref.at[my_dp], sa.at[k], ra.at[k], "dp", target)
            for k, target in others("dp", n_dp)]
    kept_here = pltpu.make_async_copy(rows_of(my_dp), mine_ref.at[my_dp], local_sem)
    kept_here.start()
    landed[my_col] = part_ref[my_col]
    wait_all(partial)
    own[...] = total_of(landed, n_col).astype(own.dtype)
    gathered = [send(own, all_ref.at[my_dp], sd.at[k], rd.at[k], "dp", target)
                for k, target in others("dp", n_dp)]
    all_ref[my_dp] = own[...]
    wait_all(gathered)
    kept_here.wait()
    wait_all(rows)


def first_exchange(activ, parts, n_dp, n_col):
    tok, width = activ.shape
    piece = parts.shape[1:]
    dma = pltpu.SemaphoreType.DMA
    return pl.pallas_call(
        functools.partial(first_kernel, n_dp, n_col),
        out_shape=(jax.ShapeDtypeStruct((n_dp, tok, width // n_dp), activ.dtype),
                   jax.ShapeDtypeStruct((n_dp,) + piece, jnp.bfloat16)),
        in_specs=[pl.BlockSpec(memory_space=pl.ANY), pl.BlockSpec(memory_space=pltpu.VMEM)],
        out_specs=(pl.BlockSpec(memory_space=pl.ANY), pl.BlockSpec(memory_space=pltpu.VMEM)),
        scratch_shapes=[pltpu.VMEM((n_col,) + piece, jnp.float32), pltpu.VMEM(piece, jnp.bfloat16),
                        dma((n_dp,)), dma((n_dp,)), dma((n_col,)), dma((n_col,)),
                        dma((n_dp,)), dma((n_dp,)), dma],
        compiler_params=pltpu.CompilerParams(collective_id=0, has_side_effects=True, vmem_limit_bytes=SPACE),
    )(activ, parts)


def gram_kernel(n_dp, n_col, sketch_ref, back_ref, gram_ref, own_ref, rows, landed, part, gin, gcol,
                ss, rs, sb, rb, s1, r1, s2, r2, s3, r3):
    my_dp, my_col = lax.axis_index("dp"), lax.axis_index("col")
    wide = sketch_ref.shape[1]
    few = part.shape[1]
    greet([("dp", n_dp, 1), ("col", n_col, 1)])
    sketches = [send(sketch_ref, rows.at[my_col], ss.at[k], rs.at[k], "col", target)
                for k, target in others("col", n_col)]
    backs = [send(back_ref.at[target], landed.at[my_dp], sb.at[k], rb.at[k], "dp", target)
             for k, target in others("dp", n_dp)]
    rows[my_col] = sketch_ref[...]
    landed[my_dp] = back_ref[my_dp]
    wait_all(backs)
    own_ref[...] = total_of(landed, n_dp)
    wait_all(sketches)
    mine = sketch_ref[...]
    block = jnp.concatenate(
        [lax.dot_general(mine, rows[c], (((0,), (0,)), ((), ())), preferred_element_type=jnp.float32)
         for c in range(n_col)], axis=1)
    for d in range(n_dp):
        part[d] = block[d * few:(d + 1) * few, :]
    parts = [send(part.at[target], gin.at[my_dp], s1.at[k], r1.at[k], "dp", target)
             for k, target in others("dp", n_dp)]
    gin[my_dp] = part[my_dp]
    wait_all(parts)
    gcol[my_col] = total_of(gin, n_dp)
    spread = [send(gcol.at[my_col], gcol.at[my_col], s2.at[k], r2.at[k], "col", target)
              for k, target in others("col", n_col)]
    wait_all(spread)
    full = [send(gcol, gram_ref.at[my_dp], s3.at[k], r3.at[k], "dp", target)
            for k, target in others("dp", n_dp)]
    gram_ref[my_dp] = gcol[...]
    wait_all(full)


def gram_exchange(sketch, back, n_dp, n_col):
    rows, wide = sketch.shape
    few = wide // n_dp
    piece = back.shape[1:]
    count = wide * n_col
    dma = pltpu.SemaphoreType.DMA
    vmem = pl.BlockSpec(memory_space=pltpu.VMEM)
    gram, own = pl.pallas_call(
        functools.partial(gram_kernel, n_dp, n_col),
        out_shape=(jax.ShapeDtypeStruct((n_dp, n_col, few, count), jnp.float32),
                   jax.ShapeDtypeStruct(piece, jnp.float32)),
        in_specs=[vmem, vmem],
        out_specs=(vmem, vmem),
        scratch_shapes=[pltpu.VMEM((n_col, rows, wide), sketch.dtype), pltpu.VMEM((n_dp,) + piece, jnp.float32),
                        pltpu.VMEM((n_dp, few, count), jnp.float32), pltpu.VMEM((n_dp, few, count), jnp.float32),
                        pltpu.VMEM((n_col, few, count), jnp.float32),
                        dma((n_col,)), dma((n_col,)), dma((n_dp,)), dma((n_dp,)), dma((n_dp,)), dma((n_dp,)),
                        dma((n_col,)), dma((n_col,)), dma((n_dp,)), dma((n_dp,))],
        compiler_params=pltpu.CompilerParams(collective_id=1, has_side_effects=True, vmem_limit_bytes=SPACE),
    )(sketch, back)
    return gram.transpose(1, 0, 2, 3).reshape(count, count), own


def last_kernel(chips, tiles, left_ref, grad_ref, other_ref, out_ref, outgoing, landed, ss, rs):
    my_dp = lax.axis_index("dp")
    my_chip = my_dp // 2
    half = grad_ref.shape[0]
    rows = left_ref.shape[0] // 2
    few = rows // chips
    tile = grad_ref.shape[1] // tiles
    greet([("dp", chips, 2)])
    copies = []
    for t in range(tiles):
        at = pl.ds(t * tile, tile)
        prod = (jnp.dot(left_ref[:, :half], grad_ref[:, at], preferred_element_type=jnp.float32)
                + jnp.dot(left_ref[:, half:], other_ref[:, at], preferred_element_type=jnp.float32))
        prod = prod[:rows] + prod[rows:]
        for q in range(chips):
            outgoing[t, q] = prod[q * few:(q + 1) * few].astype(outgoing.dtype)

            @pl.when(my_chip == q)
            def _(q=q):
                out_ref[:, at] = prod[q * few:(q + 1) * few]

        for k, target in others("dp", chips, 2):
            copies.append((t, k, send(outgoing.at[t, target // 2], landed.at[t, k],
                                      ss.at[t, k], rs.at[t, k], "dp", target)))
    for t, k, copy in copies:
        copy.wait()
        at = pl.ds(t * tile, tile)
        out_ref[:, at] = out_ref[:, at] + landed[t, k].astype(jnp.float32)


def last_exchange(left, grad_out, other, chips):
    width = grad_out.shape[1]
    tiles = 4 if width % 512 == 0 else 1
    tile = width // tiles
    few = left.shape[0] // 2 // chips
    dma = pltpu.SemaphoreType.DMA
    vmem = pl.BlockSpec(memory_space=pltpu.VMEM)
    return pl.pallas_call(
        functools.partial(last_kernel, chips, tiles),
        out_shape=jax.ShapeDtypeStruct((few, width), jnp.float32),
        in_specs=[vmem, vmem, vmem],
        out_specs=vmem,
        scratch_shapes=[pltpu.VMEM((tiles, chips, few, tile), jnp.bfloat16),
                        pltpu.VMEM((tiles, chips, few, tile), jnp.bfloat16),
                        dma((tiles, chips)), dma((tiles, chips))],
        compiler_params=pltpu.CompilerParams(collective_id=2, has_side_effects=True, vmem_limit_bytes=SPACE),
    )(left, grad_out, other)


def parity_sign(common, num_bits):
    parity = jnp.zeros_like(common)
    for shift_bit in range(num_bits):
        parity = parity + jnp.bitwise_and(jnp.right_shift(common, shift_bit), 1)
    return (1 - 2 * jnp.bitwise_and(parity, 1)).astype(jnp.bfloat16)


def kept_columns(signs, kept, my_col, ff_dev, col_dev, total_cols):
    num_bits = total_cols.bit_length() - 1
    inner = math.gcd(ff_dev, 128)
    outer = ff_dev // inner
    start = my_col * col_dev + inner * lax.broadcasted_iota(jnp.int32, (outer, 1), 0)
    high = parity_sign(jnp.bitwise_and(start, kept[None, :]), num_bits)
    place = lax.broadcasted_iota(jnp.int32, (inner, 1), 0)
    low = parity_sign(jnp.bitwise_and(place, kept[None, :]), num_bits)
    own = signs[:ff_dev].astype(jnp.bfloat16).reshape(outer, inner, 1)
    return (high[:, None, :] * low[None, :, :] * own).reshape(ff_dev, kept.shape[0])


def split(values):
    top = values.astype(jnp.bfloat16)
    return top, (values - top.astype(jnp.float32)).astype(jnp.bfloat16)


def dot_f32(left, right, dims):
    return lax.dot_general(left, right, (dims, ((), ())), preferred_element_type=jnp.float32)


def per_device(activ, grad_out, signs, kept):
    col_count = lax.axis_size("col")
    my_col = lax.axis_index("col")
    ff_dev = grad_out.shape[1]
    col_dev = signs.shape[0]
    total_cols = col_dev * col_count
    dp_count = lax.axis_size("dp")
    keep_count = kept.shape[0]
    keep_col = keep_count // col_count
    keep_dev = keep_count // dp_count
    chips = dp_count // 2
    tok_dev = activ.shape[0]
    row_dev = activ.shape[1] // dp_count
    my_core = lax.rem(lax.axis_index("dp"), 2)
    swap = [(index, index ^ 1) for index in range(dp_count)]
    grad_other = lax.ppermute(grad_out, "dp", swap)
    columns = kept_columns(signs, kept, my_col, ff_dev, col_dev, total_cols)
    mixed = dot_f32(grad_out, columns, ((1,), (0,))) * (1.0 / math.sqrt(total_cols))
    mixed = mixed.reshape(tok_dev, col_count, keep_col).transpose(1, 0, 2)
    mine, mixed = first_exchange(activ, mixed, dp_count, col_count)
    mine = mine.reshape(dp_count * tok_dev, row_dev)
    mixed = mixed.reshape(dp_count * tok_dev, keep_col)
    sketch = dot_f32(mine, mixed, ((0,), (0,)))
    top, rest = split(sketch)
    back = dot_f32(mine, top, ((1,), (0,))) + dot_f32(mine, rest, ((1,), (0,)))
    gram_matrix, back = gram_exchange(top, back.reshape(dp_count, tok_dev, keep_col), dp_count, col_count)
    back = lax.all_gather(back, "col", axis=1, tiled=True)
    back = jnp.concatenate([back, lax.ppermute(back, "dp", swap)], axis=0)
    inverse = inverse_factor(gram_matrix).reshape(chips, 2, keep_dev, keep_count)
    inverse = lax.dynamic_index_in_dim(inverse, my_core, 1, keepdims=False)
    solved = dot_hi(inverse.reshape(chips * keep_dev, keep_count), back, ((1,), (1,)))
    left = jnp.concatenate(split(solved), axis=0)
    projection = last_exchange(left, grad_out, grad_other, chips)
    return (sketch, projection)


def solution(mesh):
    placed = (P("dp", None), P("dp", "col"), P("col"), P())
    return jax.shard_map(
        per_device,
        mesh=mesh,
        in_specs=placed,
        out_specs=(P("dp", "col"), P("dp", "col")),
        check_vma=False,
    )
```

```python
import functools
import math

import jax
import jax.numpy as jnp
from jax import lax
from jax.experimental import pallas as pl
from jax.experimental.pallas import tpu as pltpu
from jax.sharding import PartitionSpec as P

HI = lax.Precision.HIGHEST


def dot_hi(left, right, dims):
    return lax.dot_general(left, right, (dims, ((), ())), precision=HI,
                           preferred_element_type=jnp.float32)


def thirds(values):
    top = values.astype(jnp.bfloat16).astype(jnp.float32)
    rest = values - top
    mid = rest.astype(jnp.bfloat16).astype(jnp.float32)
    return top, mid, rest - mid


def outer_sum(left, right):
    la, lb, lc = thirds(left)
    ra, rb, rc = thirds(right)
    return lax.dot_general(
        jnp.concatenate([la, la, lb, lb, la, lc], axis=0).astype(jnp.bfloat16),
        jnp.concatenate([ra, rb, ra, rb, rc, ra], axis=0).astype(jnp.bfloat16),
        (((0,), (0,)), ((), ())), preferred_element_type=jnp.float32)


def factor_block(both_ref):
    size = both_ref.shape[0]
    lane = lax.broadcasted_iota(jnp.int32, (8, size), 1)
    sub = lax.broadcasted_iota(jnp.int32, (8, size), 0)

    for p in range(size // 8):
        lo = 8 * p
        rows = both_ref[lo:lo + 8, :]
        rw, rv = rows[:, :size], rows[:, size:]
        cols = [jnp.broadcast_to(rw[:, lo + a:lo + a + 1], (8, size)) for a in range(8)]
        for a in range(8):
            pivot = jnp.broadcast_to(cols[a][a:a + 1, :], (8, size))
            root = lax.rsqrt(pivot)
            mult = jnp.where(sub > a, cols[a] * (root * root), jnp.where(sub == a, 1.0 - root, 0.0))
            for b in range(a + 1, 8):
                cols[b] = cols[b] - mult * jnp.broadcast_to(cols[b][a:a + 1, :], (8, size))
            rw = rw - mult * jnp.broadcast_to(rw[a:a + 1, :], (8, size))
            rv = rv - mult * jnp.broadcast_to(rv[a:a + 1, :], (8, size))
        done = jnp.concatenate([rw, rv], axis=1)
        both_ref[lo:lo + 8, :] = done
        if lo + 8 < size:
            step = outer_sum(jnp.where(lane >= lo + 8, rw, 0.0), done)
            both_ref[lo + 8:, :] = both_ref[lo + 8:, :] - step[lo + 8:, :]


def inverse_factor_kernel(gram_ref, out_ref, work, both):
    count = gram_ref.shape[0]
    size = both.shape[0]
    blocks = count // size
    row = lax.broadcasted_iota(jnp.int32, (count, count), 0)
    col = lax.broadcasted_iota(jnp.int32, (count, count), 1)
    gram = gram_ref[...]
    trace = jnp.sum(jnp.where(row == col, gram, 0.0))
    work[...] = gram + jnp.where(row == col, 0.05 * trace / count, 0.0)
    out_ref[...] = jnp.zeros_like(out_ref)
    eye = (lax.broadcasted_iota(jnp.int32, (size, size), 0)
           == lax.broadcasted_iota(jnp.int32, (size, size), 1)).astype(jnp.float32)
    for k in range(blocks):
        lo, hi = k * size, (k + 1) * size
        both[:, :size] = work[lo:hi, lo:hi]
        both[:, size:] = eye
        factor_block(both)
        inv = both[:, size:]
        if k:
            out_ref[lo:hi, :lo] = dot_hi(inv, out_ref[lo:hi, :lo], ((1,), (0,)))
        out_ref[lo:hi, lo:hi] = inv
        if hi < count:
            panel = dot_hi(inv, work[lo:hi, hi:], ((1,), (0,)))
            work[hi:, hi:] = work[hi:, hi:] - dot_hi(panel, panel, ((0,), (0,)))
            out_ref[hi:, :hi] = out_ref[hi:, :hi] - dot_hi(panel, out_ref[lo:hi, :hi], ((0,), (0,)))


def inverse_factor(gram):
    count = gram.shape[0]
    size = 128
    return pl.pallas_call(
        inverse_factor_kernel,
        out_shape=jax.ShapeDtypeStruct((count, count), jnp.float32),
        in_specs=[pl.BlockSpec(memory_space=pltpu.VMEM)],
        out_specs=pl.BlockSpec(memory_space=pltpu.VMEM),
        scratch_shapes=[pltpu.VMEM((count, count), jnp.float32),
                        pltpu.VMEM((size, 2 * size), jnp.float32)],
        compiler_params=pltpu.CompilerParams(vmem_limit_bytes=32 * 1024 * 1024),
        cost_estimate=pl.CostEstimate(flops=4 * 10**10, bytes_accessed=2 * 10**6, transcendentals=4096),
    )(gram)


MESH = pl.DeviceIdType.MESH
SPACE = 48 * 1024 * 1024


def others(axis, count, stride=1):
    me = lax.axis_index(axis)
    total = count * stride
    for offset in range(1, count):
        yield offset, lax.rem(me + offset * stride, total)


def greet(groups):
    barrier = pltpu.get_barrier_semaphore()
    waits = 0
    for axis, count, stride in groups:
        for _, target in others(axis, count, stride):
            pl.semaphore_signal(barrier, inc=1, device_id={axis: target}, device_id_type=MESH)
            waits += 1
    pl.semaphore_wait(barrier, waits)


def send(source, target_ref, send_sem, recv_sem, axis, target):
    copy = pltpu.make_async_remote_copy(
        src_ref=source, dst_ref=target_ref, send_sem=send_sem, recv_sem=recv_sem,
        device_id={axis: target}, device_id_type=MESH)
    copy.start()
    return copy


def wait_all(copies):
    for copy in copies:
        copy.wait()


def total_of(ref, count):
    total = ref[0].astype(jnp.float32)
    for index in range(1, count):
        total = total + ref[index].astype(jnp.float32)
    return total


def first_kernel(n_dp, n_col, act_ref, part_ref, out_ref, landed, outgoing, arrived, sc, rc, sd, rd):
    my_dp, my_col = lax.axis_index("dp"), lax.axis_index("col")
    wide = out_ref.shape[0]
    greet([("dp", n_dp, 1), ("col", n_col, 1)])
    partial = [send(part_ref.at[target], landed.at[my_col], sc.at[k], rc.at[k], "col", target)
               for k, target in others("col", n_col)]
    landed[my_col] = part_ref[my_col]
    wait_all(partial)
    mixed = total_of(landed, n_col)
    width = mixed.shape[1]
    top = mixed.astype(jnp.bfloat16)
    rest = (mixed - top.astype(jnp.float32)).astype(jnp.bfloat16)
    both = jnp.concatenate([top, rest], axis=1)

    def rows_of(device):
        rows = act_ref[:, pl.ds(pl.multiple_of(device * wide, wide), wide)]
        prod = lax.dot_general(rows, both, (((0,), (0,)), ((), ())), preferred_element_type=jnp.float32)
        return prod[:, :width] + prod[:, width:]

    copies = []
    for k, target in others("dp", n_dp):
        outgoing[k] = rows_of(target).astype(outgoing.dtype)
        copies.append(send(outgoing.at[k], arrived.at[k], sd.at[k], rd.at[k], "dp", target))
    out_ref[...] = rows_of(my_dp)
    wait_all(copies)
    total = out_ref[...]
    for k in range(1, n_dp):
        total = total + arrived[k].astype(jnp.float32)
    out_ref[...] = total


def first_exchange(activ, parts, n_dp, n_col):
    wide = activ.shape[1] // n_dp
    piece = parts.shape[1:]
    dma = pltpu.SemaphoreType.DMA
    vmem = pl.BlockSpec(memory_space=pltpu.VMEM)
    return pl.pallas_call(
        functools.partial(first_kernel, n_dp, n_col),
        out_shape=jax.ShapeDtypeStruct((wide, piece[1]), jnp.float32),
        in_specs=[vmem, vmem],
        out_specs=vmem,
        scratch_shapes=[pltpu.VMEM((n_col,) + piece, jnp.float32),
                        pltpu.VMEM((n_dp, wide, piece[1]), jnp.bfloat16),
                        pltpu.VMEM((n_dp, wide, piece[1]), jnp.bfloat16),
                        dma((n_col,)), dma((n_col,)), dma((n_dp,)), dma((n_dp,))],
        compiler_params=pltpu.CompilerParams(collective_id=0, has_side_effects=True, vmem_limit_bytes=SPACE),
    )(activ, parts)


def gram_kernel(n_dp, n_col, sketch_ref, gram_ref, all_ref, rows, part, gin, gcol,
                ss, rs, sb, rb, s1, r1, s2, r2, s3, r3):
    my_dp, my_col = lax.axis_index("dp"), lax.axis_index("col")
    wide = sketch_ref.shape[1]
    few = part.shape[1]
    greet([("dp", n_dp, 1), ("col", n_col, 1)])
    sketches = [send(sketch_ref, rows.at[my_col], ss.at[k], rs.at[k], "col", target)
                for k, target in others("col", n_col)]
    shared = [send(sketch_ref, all_ref.at[my_dp], sb.at[k], rb.at[k], "dp", target)
              for k, target in others("dp", n_dp)]
    rows[my_col] = sketch_ref[...]
    all_ref[my_dp] = sketch_ref[...]
    wait_all(sketches)
    mine = sketch_ref[...]
    block = jnp.concatenate(
        [lax.dot_general(mine, rows[c], (((0,), (0,)), ((), ())), preferred_element_type=jnp.float32)
         for c in range(n_col)], axis=1)
    for d in range(n_dp):
        part[d] = block[d * few:(d + 1) * few, :]
    parts = [send(part.at[target], gin.at[my_dp], s1.at[k], r1.at[k], "dp", target)
             for k, target in others("dp", n_dp)]
    gin[my_dp] = part[my_dp]
    wait_all(parts)
    gcol[my_col] = total_of(gin, n_dp)
    spread = [send(gcol.at[my_col], gcol.at[my_col], s2.at[k], r2.at[k], "col", target)
              for k, target in others("col", n_col)]
    wait_all(spread)
    full = [send(gcol, gram_ref.at[my_dp], s3.at[k], r3.at[k], "dp", target)
            for k, target in others("dp", n_dp)]
    gram_ref[my_dp] = gcol[...]
    wait_all(full)
    wait_all(shared)


def gram_exchange(sketch, n_dp, n_col):
    rows, wide = sketch.shape
    few = wide // n_dp
    count = wide * n_col
    dma = pltpu.SemaphoreType.DMA
    vmem = pl.BlockSpec(memory_space=pltpu.VMEM)
    gram, gathered = pl.pallas_call(
        functools.partial(gram_kernel, n_dp, n_col),
        out_shape=(jax.ShapeDtypeStruct((n_dp, n_col, few, count), jnp.float32),
                   jax.ShapeDtypeStruct((n_dp, rows, wide), sketch.dtype)),
        in_specs=[vmem],
        out_specs=(vmem, vmem),
        scratch_shapes=[pltpu.VMEM((n_col, rows, wide), sketch.dtype),
                        pltpu.VMEM((n_dp, few, count), jnp.float32), pltpu.VMEM((n_dp, few, count), jnp.float32),
                        pltpu.VMEM((n_col, few, count), jnp.float32),
                        dma((n_col,)), dma((n_col,)), dma((n_dp,)), dma((n_dp,)), dma((n_dp,)), dma((n_dp,)),
                        dma((n_col,)), dma((n_col,)), dma((n_dp,)), dma((n_dp,))],
        compiler_params=pltpu.CompilerParams(collective_id=1, has_side_effects=True, vmem_limit_bytes=SPACE),
    )(sketch)
    return gram.transpose(1, 0, 2, 3).reshape(count, count), gathered.reshape(n_dp * rows, wide)


def last_kernel(chips, tiles, left_ref, grad_ref, other_ref, out_ref, outgoing, landed, ss, rs):
    my_dp = lax.axis_index("dp")
    my_chip = my_dp // 2
    half = grad_ref.shape[0]
    rows = left_ref.shape[0] // 2
    few = rows // chips
    tile = grad_ref.shape[1] // tiles
    greet([("dp", chips, 2)])
    copies = []
    for t in range(tiles):
        at = pl.ds(t * tile, tile)
        prod = (jnp.dot(left_ref[:, :half], grad_ref[:, at], preferred_element_type=jnp.float32)
                + jnp.dot(left_ref[:, half:], other_ref[:, at], preferred_element_type=jnp.float32))
        prod = prod[:rows] + prod[rows:]
        for q in range(chips):
            outgoing[t, q] = prod[q * few:(q + 1) * few].astype(outgoing.dtype)

            @pl.when(my_chip == q)
            def _(q=q):
                out_ref[:, at] = prod[q * few:(q + 1) * few]

        for k, target in others("dp", chips, 2):
            copies.append((t, k, send(outgoing.at[t, target // 2], landed.at[t, k],
                                      ss.at[t, k], rs.at[t, k], "dp", target)))
    for t, k, copy in copies:
        copy.wait()
        at = pl.ds(t * tile, tile)
        out_ref[:, at] = out_ref[:, at] + landed[t, k].astype(jnp.float32)


def last_exchange(left, grad_out, other, chips):
    width = grad_out.shape[1]
    tiles = 4 if width % 512 == 0 else 1
    tile = width // tiles
    few = left.shape[0] // 2 // chips
    dma = pltpu.SemaphoreType.DMA
    vmem = pl.BlockSpec(memory_space=pltpu.VMEM)
    return pl.pallas_call(
        functools.partial(last_kernel, chips, tiles),
        out_shape=jax.ShapeDtypeStruct((few, width), jnp.float32),
        in_specs=[vmem, vmem, vmem],
        out_specs=vmem,
        scratch_shapes=[pltpu.VMEM((tiles, chips, few, tile), jnp.bfloat16),
                        pltpu.VMEM((tiles, chips, few, tile), jnp.bfloat16),
                        dma((tiles, chips)), dma((tiles, chips))],
        compiler_params=pltpu.CompilerParams(collective_id=2, has_side_effects=True, vmem_limit_bytes=SPACE),
    )(left, grad_out, other)


def parity_sign(common, num_bits):
    parity = jnp.zeros_like(common)
    for shift_bit in range(num_bits):
        parity = parity + jnp.bitwise_and(jnp.right_shift(common, shift_bit), 1)
    return (1 - 2 * jnp.bitwise_and(parity, 1)).astype(jnp.bfloat16)


def kept_columns(signs, kept, my_col, ff_dev, col_dev, total_cols):
    num_bits = total_cols.bit_length() - 1
    inner = math.gcd(ff_dev, 128)
    outer = ff_dev // inner
    start = my_col * col_dev + inner * lax.broadcasted_iota(jnp.int32, (outer, 1), 0)
    high = parity_sign(jnp.bitwise_and(start, kept[None, :]), num_bits)
    place = lax.broadcasted_iota(jnp.int32, (inner, 1), 0)
    low = parity_sign(jnp.bitwise_and(place, kept[None, :]), num_bits)
    own = signs[:ff_dev].astype(jnp.bfloat16).reshape(outer, inner, 1)
    return (high[:, None, :] * low[None, :, :] * own).reshape(ff_dev, kept.shape[0])


def split(values):
    top = values.astype(jnp.bfloat16)
    return top, (values - top.astype(jnp.float32)).astype(jnp.bfloat16)


def dot_f32(left, right, dims):
    return lax.dot_general(left, right, (dims, ((), ())), preferred_element_type=jnp.float32)


def per_device(activ, grad_out, signs, kept):
    col_count = lax.axis_size("col")
    my_col = lax.axis_index("col")
    ff_dev = grad_out.shape[1]
    col_dev = signs.shape[0]
    total_cols = col_dev * col_count
    dp_count = lax.axis_size("dp")
    keep_count = kept.shape[0]
    keep_col = keep_count // col_count
    keep_dev = keep_count // dp_count
    chips = dp_count // 2
    tok_dev = activ.shape[0]
    my_core = lax.rem(lax.axis_index("dp"), 2)
    swap = [(index, index ^ 1) for index in range(dp_count)]
    act_other = lax.ppermute(activ, "dp", swap)
    grad_other = lax.ppermute(grad_out, "dp", swap)
    columns = kept_columns(signs, kept, my_col, ff_dev, col_dev, total_cols)
    mixed = dot_f32(grad_out, columns, ((1,), (0,))) * (1.0 / math.sqrt(total_cols))
    mixed = mixed.reshape(tok_dev, col_count, keep_col).transpose(1, 0, 2)
    sketch = first_exchange(activ, mixed, dp_count, col_count)
    gram_matrix, rounded = gram_exchange(sketch.astype(jnp.bfloat16), dp_count, col_count)
    own = dot_f32(jnp.concatenate([activ, act_other], axis=0), rounded, ((1,), (0,)))
    back = jnp.zeros((2 * tok_dev, keep_count), jnp.float32)
    for offset in range(col_count):
        piece = own
        if offset:
            piece = lax.ppermute(own, "col", [(c, (c + offset) % col_count) for c in range(col_count)])
        place = lax.rem(my_col - offset + col_count, col_count) * keep_col
        back = lax.dynamic_update_slice(back, piece, (0, place))
    inverse = inverse_factor(gram_matrix).reshape(chips, 2, keep_dev, keep_count)
    inverse = lax.dynamic_index_in_dim(inverse, my_core, 1, keepdims=False)
    solved = dot_hi(inverse.reshape(chips * keep_dev, keep_count), back, ((1,), (1,)))
    left = jnp.concatenate(split(solved), axis=0)
    projection = last_exchange(left, grad_out, grad_other, chips)
    return (sketch, projection)


def solution(mesh):
    placed = (P("dp", None), P("dp", "col"), P("col"), P())
    return jax.shard_map(
        per_device,
        mesh=mesh,
        in_specs=placed,
        out_specs=(P("dp", "col"), P("dp", "col")),
        check_vma=False,
    )
```

```python
import functools
import math

import jax
import jax.numpy as jnp
from jax import lax
from jax.experimental import pallas as pl
from jax.experimental.pallas import tpu as pltpu
from jax.sharding import PartitionSpec as P

HI = lax.Precision.HIGHEST


def dot_hi(left, right, dims):
    return lax.dot_general(left, right, (dims, ((), ())), precision=HI,
                           preferred_element_type=jnp.float32)


def thirds(values):
    top = values.astype(jnp.bfloat16).astype(jnp.float32)
    rest = values - top
    mid = rest.astype(jnp.bfloat16).astype(jnp.float32)
    return top, mid, rest - mid


def outer_sum(left, right):
    la, lb, lc = thirds(left)
    ra, rb, rc = thirds(right)
    return lax.dot_general(
        jnp.concatenate([la, la, lb, lb, la, lc], axis=0).astype(jnp.bfloat16),
        jnp.concatenate([ra, rb, ra, rb, rc, ra], axis=0).astype(jnp.bfloat16),
        (((0,), (0,)), ((), ())), preferred_element_type=jnp.float32)


def factor_block(both_ref):
    size = both_ref.shape[0]
    lane = lax.broadcasted_iota(jnp.int32, (8, size), 1)
    sub = lax.broadcasted_iota(jnp.int32, (8, size), 0)

    for p in range(size // 8):
        lo = 8 * p
        rows = both_ref[lo:lo + 8, :]
        rw, rv = rows[:, :size], rows[:, size:]
        cols = [jnp.broadcast_to(rw[:, lo + a:lo + a + 1], (8, size)) for a in range(8)]
        for a in range(8):
            pivot = jnp.broadcast_to(cols[a][a:a + 1, :], (8, size))
            root = lax.rsqrt(pivot)
            mult = jnp.where(sub > a, cols[a] * (root * root), jnp.where(sub == a, 1.0 - root, 0.0))
            for b in range(a + 1, 8):
                cols[b] = cols[b] - mult * jnp.broadcast_to(cols[b][a:a + 1, :], (8, size))
            rw = rw - mult * jnp.broadcast_to(rw[a:a + 1, :], (8, size))
            rv = rv - mult * jnp.broadcast_to(rv[a:a + 1, :], (8, size))
        done = jnp.concatenate([rw, rv], axis=1)
        both_ref[lo:lo + 8, :] = done
        if lo + 8 < size:
            step = outer_sum(jnp.where(lane >= lo + 8, rw, 0.0), done)
            both_ref[lo + 8:, :] = both_ref[lo + 8:, :] - step[lo + 8:, :]


def inverse_factor_kernel(gram_ref, out_ref, work, both):
    count = gram_ref.shape[0]
    size = both.shape[0]
    blocks = count // size
    row = lax.broadcasted_iota(jnp.int32, (count, count), 0)
    col = lax.broadcasted_iota(jnp.int32, (count, count), 1)
    gram = gram_ref[...]
    trace = jnp.sum(jnp.where(row == col, gram, 0.0))
    work[...] = gram + jnp.where(row == col, 0.05 * trace / count, 0.0)
    out_ref[...] = jnp.zeros_like(out_ref)
    eye = (lax.broadcasted_iota(jnp.int32, (size, size), 0)
           == lax.broadcasted_iota(jnp.int32, (size, size), 1)).astype(jnp.float32)
    for k in range(blocks):
        lo, hi = k * size, (k + 1) * size
        both[:, :size] = work[lo:hi, lo:hi]
        both[:, size:] = eye
        factor_block(both)
        inv = both[:, size:]
        if k:
            out_ref[lo:hi, :lo] = dot_hi(inv, out_ref[lo:hi, :lo], ((1,), (0,)))
        out_ref[lo:hi, lo:hi] = inv
        if hi < count:
            panel = dot_hi(inv, work[lo:hi, hi:], ((1,), (0,)))
            work[hi:, hi:] = work[hi:, hi:] - dot_hi(panel, panel, ((0,), (0,)))
            out_ref[hi:, :hi] = out_ref[hi:, :hi] - dot_hi(panel, out_ref[lo:hi, :hi], ((0,), (0,)))


def inverse_factor(gram):
    count = gram.shape[0]
    size = 128
    return pl.pallas_call(
        inverse_factor_kernel,
        out_shape=jax.ShapeDtypeStruct((count, count), jnp.float32),
        in_specs=[pl.BlockSpec(memory_space=pltpu.VMEM)],
        out_specs=pl.BlockSpec(memory_space=pltpu.VMEM),
        scratch_shapes=[pltpu.VMEM((count, count), jnp.float32),
                        pltpu.VMEM((size, 2 * size), jnp.float32)],
        compiler_params=pltpu.CompilerParams(vmem_limit_bytes=32 * 1024 * 1024),
        cost_estimate=pl.CostEstimate(flops=4 * 10**10, bytes_accessed=2 * 10**6, transcendentals=4096),
    )(gram)


MESH = pl.DeviceIdType.MESH
SPACE = 48 * 1024 * 1024


def others(axis, count, stride=1):
    me = lax.axis_index(axis)
    total = count * stride
    for offset in range(1, count):
        yield offset, lax.rem(me + offset * stride, total)


def greet(groups):
    barrier = pltpu.get_barrier_semaphore()
    waits = 0
    for axis, count, stride in groups:
        for _, target in others(axis, count, stride):
            pl.semaphore_signal(barrier, inc=1, device_id={axis: target}, device_id_type=MESH)
            waits += 1
    pl.semaphore_wait(barrier, waits)


def send(source, target_ref, send_sem, recv_sem, axis, target):
    copy = pltpu.make_async_remote_copy(
        src_ref=source, dst_ref=target_ref, send_sem=send_sem, recv_sem=recv_sem,
        device_id={axis: target}, device_id_type=MESH)
    copy.start()
    return copy


def wait_all(copies):
    for copy in copies:
        copy.wait()


def gather_pairs(source, target_ref, count, sems):
    s1, r1, s2, r2 = sems
    me = lax.axis_index("dp")
    partner = me + 1 - 2 * lax.rem(me, 2)
    first = [(k, send(source, target_ref.at[me], s1.at[k], r1.at[k], "dp", target))
             for k, target in others("dp", count // 2, 2)]
    second = [send(source, target_ref.at[me], s2.at[0], r2.at[0], "dp", partner)]

    def finish():
        for k, copy in first:
            copy.wait()
            origin = lax.rem(me - 2 * k + count, count)
            second.append(send(target_ref.at[origin], target_ref.at[origin], s2.at[k], r2.at[k], "dp", partner))
        wait_all(second)

    return finish


def total_of(ref, count):
    total = ref[0].astype(jnp.float32)
    for index in range(1, count):
        total = total + ref[index].astype(jnp.float32)
    return total


def first_kernel(n_dp, n_col, act_ref, part_ref, out_ref, landed, outgoing, arrived, sc, rc, sd, rd):
    my_dp, my_col = lax.axis_index("dp"), lax.axis_index("col")
    wide = out_ref.shape[0]
    greet([("dp", n_dp, 1), ("col", n_col, 1)])
    partial = [send(part_ref.at[target], landed.at[my_col], sc.at[k], rc.at[k], "col", target)
               for k, target in others("col", n_col)]
    landed[my_col] = part_ref[my_col]
    wait_all(partial)
    mixed = total_of(landed, n_col)
    width = mixed.shape[1]
    top = mixed.astype(jnp.bfloat16)
    rest = (mixed - top.astype(jnp.float32)).astype(jnp.bfloat16)
    both = jnp.concatenate([top, rest], axis=1)

    def rows_of(device):
        rows = act_ref[:, pl.ds(pl.multiple_of(device * wide, wide), wide)]
        prod = lax.dot_general(rows, both, (((0,), (0,)), ((), ())), preferred_element_type=jnp.float32)
        return prod[:, :width] + prod[:, width:]

    copies = []
    for k, target in others("dp", n_dp):
        outgoing[k] = rows_of(target).astype(outgoing.dtype)
        copies.append(send(outgoing.at[k], arrived.at[k], sd.at[k], rd.at[k], "dp", target))
    out_ref[...] = rows_of(my_dp)
    wait_all(copies)
    total = out_ref[...]
    for k in range(1, n_dp):
        total = total + arrived[k].astype(jnp.float32)
    out_ref[...] = total


def first_exchange(activ, parts, n_dp, n_col):
    wide = activ.shape[1] // n_dp
    piece = parts.shape[1:]
    dma = pltpu.SemaphoreType.DMA
    vmem = pl.BlockSpec(memory_space=pltpu.VMEM)
    return pl.pallas_call(
        functools.partial(first_kernel, n_dp, n_col),
        out_shape=jax.ShapeDtypeStruct((wide, piece[1]), jnp.float32),
        in_specs=[vmem, vmem],
        out_specs=vmem,
        scratch_shapes=[pltpu.VMEM((n_col,) + piece, jnp.bfloat16),
                        pltpu.VMEM((n_dp, wide, piece[1]), jnp.bfloat16),
                        pltpu.VMEM((n_dp, wide, piece[1]), jnp.bfloat16),
                        dma((n_col,)), dma((n_col,)), dma((n_dp,)), dma((n_dp,))],
        compiler_params=pltpu.CompilerParams(collective_id=0, has_side_effects=True, vmem_limit_bytes=SPACE),
    )(activ, parts)


def gram_kernel(n_dp, n_col, sketch_ref, gram_ref, all_ref, rows, part, gin, gcol,
                ss, rs, sb, rb, s1, r1, s2, r2, s3, r3, sf, rf, s4, r4):
    my_dp, my_col = lax.axis_index("dp"), lax.axis_index("col")
    wide = sketch_ref.shape[1]
    few = part.shape[1]
    greet([("dp", n_dp, 1), ("col", n_col, 1)])
    sketches = [send(sketch_ref, rows.at[my_col], ss.at[k], rs.at[k], "col", target)
                for k, target in others("col", n_col)]
    shared = gather_pairs(sketch_ref, all_ref, n_dp, (sb, rb, sf, rf))
    rows[my_col] = sketch_ref[...]
    all_ref[my_dp] = sketch_ref[...]
    wait_all(sketches)
    mine = sketch_ref[...]
    block = jnp.concatenate(
        [lax.dot_general(mine, rows[c], (((0,), (0,)), ((), ())), preferred_element_type=jnp.float32)
         for c in range(n_col)], axis=1)
    for d in range(n_dp):
        part[d] = block[d * few:(d + 1) * few, :]
    parts = [send(part.at[target], gin.at[my_dp], s1.at[k], r1.at[k], "dp", target)
             for k, target in others("dp", n_dp)]
    gin[my_dp] = part[my_dp]
    wait_all(parts)
    gcol[my_col] = total_of(gin, n_dp)
    spread = [send(gcol.at[my_col], gcol.at[my_col], s2.at[k], r2.at[k], "col", target)
              for k, target in others("col", n_col)]
    wait_all(spread)
    full = gather_pairs(gcol, gram_ref, n_dp, (s3, r3, s4, r4))
    gram_ref[my_dp] = gcol[...]
    shared()
    full()


def gram_exchange(sketch, n_dp, n_col):
    rows, wide = sketch.shape
    few = wide // n_dp
    count = wide * n_col
    dma = pltpu.SemaphoreType.DMA
    vmem = pl.BlockSpec(memory_space=pltpu.VMEM)
    gram, gathered = pl.pallas_call(
        functools.partial(gram_kernel, n_dp, n_col),
        out_shape=(jax.ShapeDtypeStruct((n_dp, n_col, few, count), jnp.float32),
                   jax.ShapeDtypeStruct((n_dp, rows, wide), sketch.dtype)),
        in_specs=[vmem],
        out_specs=(vmem, vmem),
        scratch_shapes=[pltpu.VMEM((n_col, rows, wide), sketch.dtype),
                        pltpu.VMEM((n_dp, few, count), jnp.float32), pltpu.VMEM((n_dp, few, count), jnp.float32),
                        pltpu.VMEM((n_col, few, count), jnp.float32),
                        dma((n_col,)), dma((n_col,)), dma((n_dp,)), dma((n_dp,)), dma((n_dp,)), dma((n_dp,)),
                        dma((n_col,)), dma((n_col,)), dma((n_dp,)), dma((n_dp,)),
                        dma((n_dp,)), dma((n_dp,)), dma((n_dp,)), dma((n_dp,))],
        compiler_params=pltpu.CompilerParams(collective_id=1, has_side_effects=True, vmem_limit_bytes=SPACE),
    )(sketch)
    return gram.transpose(1, 0, 2, 3).reshape(count, count), gathered.reshape(n_dp * rows, wide)


def last_kernel(chips, tiles, left_ref, grad_ref, other_ref, out_ref, outgoing, landed, ss, rs):
    my_dp = lax.axis_index("dp")
    my_chip = my_dp // 2
    half = grad_ref.shape[0]
    rows = left_ref.shape[0] // 2
    few = rows // chips
    tile = grad_ref.shape[1] // tiles
    greet([("dp", chips, 2)])
    copies = []
    for t in range(tiles):
        at = pl.ds(t * tile, tile)
        prod = (jnp.dot(left_ref[:, :half], grad_ref[:, at], preferred_element_type=jnp.float32)
                + jnp.dot(left_ref[:, half:], other_ref[:, at], preferred_element_type=jnp.float32))
        prod = prod[:rows] + prod[rows:]
        for q in range(chips):
            outgoing[t, q] = prod[q * few:(q + 1) * few].astype(outgoing.dtype)

            @pl.when(my_chip == q)
            def _(q=q):
                out_ref[:, at] = prod[q * few:(q + 1) * few]

        for k, target in others("dp", chips, 2):
            copies.append((t, k, send(outgoing.at[t, target // 2], landed.at[t, k],
                                      ss.at[t, k], rs.at[t, k], "dp", target)))
    for t, k, copy in copies:
        copy.wait()
        at = pl.ds(t * tile, tile)
        out_ref[:, at] = out_ref[:, at] + landed[t, k].astype(jnp.float32)


def last_exchange(left, grad_out, other, chips):
    width = grad_out.shape[1]
    tiles = 4 if width % 512 == 0 else 1
    tile = width // tiles
    few = left.shape[0] // 2 // chips
    dma = pltpu.SemaphoreType.DMA
    vmem = pl.BlockSpec(memory_space=pltpu.VMEM)
    return pl.pallas_call(
        functools.partial(last_kernel, chips, tiles),
        out_shape=jax.ShapeDtypeStruct((few, width), jnp.float32),
        in_specs=[vmem, vmem, vmem],
        out_specs=vmem,
        scratch_shapes=[pltpu.VMEM((tiles, chips, few, tile), jnp.bfloat16),
                        pltpu.VMEM((tiles, chips, few, tile), jnp.bfloat16),
                        dma((tiles, chips)), dma((tiles, chips))],
        compiler_params=pltpu.CompilerParams(collective_id=2, has_side_effects=True, vmem_limit_bytes=SPACE),
    )(left, grad_out, other)


def parity_sign(common, num_bits):
    parity = jnp.zeros_like(common)
    for shift_bit in range(num_bits):
        parity = parity + jnp.bitwise_and(jnp.right_shift(common, shift_bit), 1)
    return (1 - 2 * jnp.bitwise_and(parity, 1)).astype(jnp.bfloat16)


def kept_columns(signs, kept, my_col, ff_dev, col_dev, total_cols):
    num_bits = total_cols.bit_length() - 1
    inner = math.gcd(ff_dev, 128)
    outer = ff_dev // inner
    start = my_col * col_dev + inner * lax.broadcasted_iota(jnp.int32, (outer, 1), 0)
    high = parity_sign(jnp.bitwise_and(start, kept[None, :]), num_bits)
    place = lax.broadcasted_iota(jnp.int32, (inner, 1), 0)
    low = parity_sign(jnp.bitwise_and(place, kept[None, :]), num_bits)
    own = signs[:ff_dev].astype(jnp.bfloat16).reshape(outer, inner, 1)
    return (high[:, None, :] * low[None, :, :] * own).reshape(ff_dev, kept.shape[0])


def split(values):
    top = values.astype(jnp.bfloat16)
    return top, (values - top.astype(jnp.float32)).astype(jnp.bfloat16)


def dot_f32(left, right, dims):
    return lax.dot_general(left, right, (dims, ((), ())), preferred_element_type=jnp.float32)


def per_device(activ, grad_out, signs, kept):
    col_count = lax.axis_size("col")
    my_col = lax.axis_index("col")
    ff_dev = grad_out.shape[1]
    col_dev = signs.shape[0]
    total_cols = col_dev * col_count
    dp_count = lax.axis_size("dp")
    keep_count = kept.shape[0]
    keep_col = keep_count // col_count
    keep_dev = keep_count // dp_count
    chips = dp_count // 2
    tok_dev = activ.shape[0]
    my_core = lax.rem(lax.axis_index("dp"), 2)
    swap = [(index, index ^ 1) for index in range(dp_count)]
    act_other = lax.ppermute(activ, "dp", swap)
    grad_other = lax.ppermute(grad_out, "dp", swap)
    columns = kept_columns(signs, kept, my_col, ff_dev, col_dev, total_cols)
    mixed = dot_f32(grad_out, columns, ((1,), (0,))) * (1.0 / math.sqrt(total_cols))
    mixed = mixed.reshape(tok_dev, col_count, keep_col).transpose(1, 0, 2)
    sketch = first_exchange(activ, mixed.astype(jnp.bfloat16), dp_count, col_count)
    gram_matrix, rounded = gram_exchange(sketch.astype(jnp.bfloat16), dp_count, col_count)
    own = dot_f32(jnp.concatenate([activ, act_other], axis=0), rounded, ((1,), (0,)))
    back = jnp.zeros((2 * tok_dev, keep_count), jnp.float32)
    for offset in range(col_count):
        piece = own
        if offset:
            piece = lax.ppermute(own, "col", [(c, (c + offset) % col_count) for c in range(col_count)])
        place = lax.rem(my_col - offset + col_count, col_count) * keep_col
        back = lax.dynamic_update_slice(back, piece, (0, place))
    inverse = inverse_factor(gram_matrix).reshape(chips, 2, keep_dev, keep_count)
    inverse = lax.dynamic_index_in_dim(inverse, my_core, 1, keepdims=False)
    solved = dot_hi(inverse.reshape(chips * keep_dev, keep_count), back, ((1,), (1,)))
    left = jnp.concatenate(split(solved), axis=0)
    projection = last_exchange(left, grad_out, grad_other, chips)
    return (sketch, projection)


def solution(mesh):
    placed = (P("dp", None), P("dp", "col"), P("col"), P())
    return jax.shard_map(
        per_device,
        mesh=mesh,
        in_specs=placed,
        out_specs=(P("dp", "col"), P("dp", "col")),
        check_vma=False,
    )
```
